32 devices in a mesh: groups: 2 (over y), mp: 4 (over x, core), embed: 4 (over z).
Axes of the slice: x: 2, y: 2, z: 4, core: 2. Of those that a mesh axis runs over, the one named last changes fastest.
Arguments:
- x_rows: bfloat16 [64, 18432], P(('groups', 'mp'), 'embed'), parts along dimension 0, may hold values from -6 to 6
- joined_weight: bfloat16 [18432, 12800], P('embed', 'mp'), may hold values from -0.046875 to 0.046875
- cache_keys: bfloat16 [64, 512, 256], P(('groups', 'mp', 'embed')), parts along dimension 0, may hold values from -384 to 384
- cache_values: bfloat16 [64, 512, 256], P(('groups', 'mp', 'embed')), parts along dimension 0, may hold values from -6 to 6
- lengths: int32 [64], P(('groups', 'mp', 'embed')), parts along dimension 0, may hold values from 1 to 512, as said below
- out_weight: bfloat16 [12288, 18432], P('mp', 'embed'), may hold values from -0.0546875 to 0.0546875
Outputs:
- layer_out: bfloat16 [64, 18432], P(('groups', 'mp'), 'embed'), parts along dimension 0
The draws below stay inside these ranges and needn't reach their ends.
There are 2 independent parts, one for each index of `groups`. The reference program is written for one: setup_inputs(seed, part) draws one part's arguments, and reference() takes and returns one part's arrays. A program takes and returns all parts, laid end to end along the dimension named above; an argument that names none is the same for every part. Nothing has to cross between parts.
Inputs may be any that keep to these rules, and one draw needn't show every extreme that they name: `lengths`: some row of every draw has exactly 512 valid positions.
All inputs are finite; a program needn't handle non-finite values.
Results may differ from the reference program's by a relative error of at most 0.012.
The reference program's roundings to bfloat16 on the way (of `projected` and `attended`) count: a program that leaves them out, or rounds other values in their place, can miss the bound.
Values may be sent and summed in bfloat16 or wider, within the bound.
A program may use at most 128 MiB of HBM per device.

```python
import math
import jax
import jax.numpy as jnp
from jax import lax

D = 18432
H = 48
DH = 256
LEN = 512
HD = 12288
JOINED = 12800
ROWS = 32


def draw_lengths(key, part):
    key = jax.random.fold_in(key, 11)
    first_key, second_key = jax.random.split(key)
    drawn = jax.random.randint(first_key, (ROWS,), 1, LEN + 1)
    chosen = jax.random.randint(second_key, (), 0, ROWS)
    return jnp.where(jnp.arange(ROWS) == chosen, LEN, drawn).astype(jnp.int32)


def draw_cache_keys(key, part):
    key = jax.random.fold_in(key, 23)
    first_key = jax.random.fold_in(key, 0)
    values = jnp.clip(jax.random.normal(first_key, (ROWS, LEN, DH), jnp.float32), -6.0, 6.0)
    return values.astype(jnp.bfloat16)


def shard_levels(rng, extent, pieces, smallest, high):
    def one(dim, blocks):
        steps = jax.random.uniform(jax.random.fold_in(jax.random.fold_in(rng, 6), dim), (blocks,), jnp.float32, smallest / len(pieces), high / len(pieces))
        return jnp.repeat(jnp.exp(steps), extent[dim] // blocks).reshape((-1,) + (1,) * (len(extent) - dim - 1))

    factor_of = one(*pieces[0])
    for cut in pieces[1:]:
        factor_of = factor_of * one(*cut)
    return factor_of


def scatter_about(stream_key, dims, deviation, reach, pieces=(), kind=jnp.bfloat16):
    entries = deviation * jax.random.normal(stream_key, dims, jnp.float32)
    if pieces:
        entries = entries * shard_levels(stream_key, dims, pieces, -0.22, 0.18)
    return jnp.clip(entries, -reach, reach).astype(kind)


def setup_inputs(seed: int = 0, part: int = 0) -> dict:
    key_of = jax.random.split(jax.random.key(seed), 7)
    own_keys = jax.random.split(jax.random.fold_in(key_of[6], part), 7)
    x_rows = scatter_about(own_keys[0], (ROWS, D), 1.0, 6.0, ((0, 4), (1, 4)))
    joined_weight = scatter_about(key_of[1], (D, JOINED), D ** -0.5, 0.046875, ((0, 4), (1, 4)))
    cache_keys = draw_cache_keys(jax.random.fold_in(jax.random.fold_in(key_of[6], part), 71), part)
    cache_values = scatter_about(own_keys[3], (ROWS, LEN, DH), 1.0, 6.0, ((0, 16),))
    lengths = draw_lengths(jax.random.fold_in(jax.random.fold_in(key_of[6], part), 71), part)
    out_weight = scatter_about(key_of[5], (HD, D), HD ** -0.5, 0.0546875, ((0, 4), (1, 4)))
    return dict(x_rows=x_rows, joined_weight=joined_weight, cache_keys=cache_keys, cache_values=cache_values, lengths=lengths, out_weight=out_weight)


def reference(x_rows, joined_weight, cache_keys, cache_values, lengths, out_weight):
    projected = jnp.dot(x_rows, joined_weight, preferred_element_type=jnp.float32).astype(jnp.bfloat16)
    queries = projected[:, :HD].reshape(ROWS, H, DH).astype(jnp.float32)
    new_key = projected[:, HD:HD + DH].astype(jnp.float32)
    new_value = projected[:, HD + DH:].astype(jnp.float32)
    score_scale = 1.0 / math.sqrt(DH)
    scores = jnp.einsum('rhd,rld->rhl', queries, cache_keys.astype(jnp.float32)) * score_scale
    new_score = jnp.einsum('rhd,rd->rh', queries, new_key) * score_scale
    visible = jnp.arange(LEN, dtype=jnp.int32)[None, None, :] < lengths.astype(jnp.int32)[:, None, None]
    scores = jnp.where(visible, scores, -1e+30)
    highest = jnp.maximum(lax.optimization_barrier(jnp.max(scores, axis=-1)), new_score)
    expo = jnp.where(visible, jnp.exp(scores - highest[..., None]), 0.0)
    new_expo = jnp.exp(new_score - highest)
    denominator = lax.optimization_barrier(jnp.sum(expo, axis=-1)) + new_expo
    weights = (expo / denominator[..., None]).astype(jnp.bfloat16)
    new_weight = (new_expo / denominator).astype(jnp.bfloat16)
    attended = jnp.einsum('rhl,rld->rhd', weights.astype(jnp.float32), cache_values.astype(jnp.float32))
    attended = attended + new_weight.astype(jnp.float32)[..., None] * new_value[:, None, :]
    attended = attended.astype(jnp.bfloat16).reshape(ROWS, HD)
    return jnp.dot(attended, out_weight, preferred_element_type=jnp.float32).astype(jnp.bfloat16)
```

```python
import functools
import math

import jax
import jax.numpy as jnp
from jax import lax
from jax.experimental import pallas as pl
from jax.experimental.pallas import tpu as pltpu
from jax.sharding import PartitionSpec as P


LANES = 128
JOINED_TILE = 512
OUT_TILE = 256
F32 = jnp.float32
BF16 = jnp.bfloat16
VMEM_BYTES = 63 * 1024 * 1024


def fused_kernel(
    sizes,
    lengths_ref,
    x_ref,
    wj_ref,
    ck_ref,
    cv_ref,
    wo_ref,
    out_ref,
    x_in,
    x_pack,
    x_all,
    lhs,
    wj,
    wo,
    keys,
    values,
    partial,
    partial_in,
    rows_out,
    rows_in,
    query,
    att,
    att_rows,
    att_out,
    att_in,
    att_f32,
    att_lhs,
    product,
    out_send,
    out_in,
    load_sem,
    wj_sem,
    wo_sem,
    x_ssem,
    x_rsem,
    b_ssem,
    b_rsem,
    c_ssem,
    c_rsem,
    d_ssem,
    d_rsem,
    f_ssem,
    f_rsem,
):
    mp, em, heads, dh, cache_len = sizes
    me = lax.axis_index("mp")
    my = lax.axis_index("embed")
    count = mp * em
    own = me * em + my
    rows_x, width = x_ref.shape
    half = width // 2
    columns = wj_ref.shape[1]
    chunks = columns // LANES
    full = columns // JOINED_TILE
    rest = columns - full * JOINED_TILE
    out_half = out_ref.shape[1] // 2
    pairs = out_half // OUT_TILE
    heads_here = heads // mp

    def remote(src, dst, ssem, rsem, p, q):
        return pltpu.make_async_remote_copy(
            src_ref=src,
            dst_ref=dst,
            send_sem=ssem,
            recv_sem=rsem,
            device_id={"mp": p, "embed": q},
            device_id_type=pl.DeviceIdType.MESH,
        )

    def tile(j, size=JOINED_TILE):
        return pl.ds(pl.multiple_of(j * JOINED_TILE, LANES), size)

    def wj_copy(j, size=JOINED_TILE):
        return pltpu.make_async_copy(wj_ref.at[:, tile(j, size)], wj.at[:, tile(j, size)], wj_sem.at[j])

    def wo_copy(j, side):
        place = pl.ds(pl.multiple_of(side * out_half + j * OUT_TILE, LANES), OUT_TILE)
        return pltpu.make_async_copy(wo_ref.at[:, place], wo.at[:, place], wo_sem.at[side, j])

    x_load = pltpu.make_async_copy(x_ref, x_in, load_sem.at[0])
    x_load.start()

    @pl.loop(0, full)
    def _(j):
        wj_copy(j).start()

    if rest:
        wj_copy(full, rest).start()
    key_load = pltpu.make_async_copy(ck_ref, keys, load_sem.at[1])
    value_load = pltpu.make_async_copy(cv_ref, values, load_sem.at[2])
    key_load.start()
    value_load.start()

    barrier = pltpu.get_barrier_semaphore()

    @pl.loop(1, count)
    def _(d):
        t = lax.rem(own + d, count)
        pl.semaphore_signal(
            barrier,
            inc=1,
            device_id={"mp": t // em, "embed": lax.rem(t, em)},
            device_id_type=pl.DeviceIdType.MESH,
        )

    x_load.wait()
    x32 = x_in[...].astype(F32)
    x_pack[...] = jnp.concatenate([x32[:, :half], x32[:, half:]], axis=0).astype(BF16)
    pl.semaphore_wait(barrier, count - 1)

    def x_slot(p):
        return x_all.at[pl.ds(pl.multiple_of(p * 2 * rows_x, 2 * rows_x), 2 * rows_x), :]

    for d in range(1, mp):
        p = lax.rem(me + d, mp)
        remote(x_pack, x_slot(me), x_ssem.at[d], x_rsem.at[me], p, my).start()
    x_slot(me)[...] = x_pack[...]
    for d in range(1, mp):
        p = lax.rem(me + d, mp)
        remote(x_pack, x_slot(p), x_ssem.at[d], x_rsem.at[p], p, my).wait_recv()

    total = mp * rows_x
    row = lax.broadcasted_iota(jnp.int32, (total, 2 * total), 0)
    col = lax.broadcasted_iota(jnp.int32, (total, 2 * total), 1)
    wanted = (lax.rem(row, 2 * mp) // 2) * (2 * rows_x) + (row // (2 * mp)) * 2 + lax.rem(row, 2)
    for side in range(2):
        pick = jnp.where(col == wanted + side * rows_x, 1.0, 0.0).astype(BF16)
        lhs[:, side * half : (side + 1) * half] = jnp.dot(
            pick, x_all[...], preferred_element_type=F32
        ).astype(BF16)

    def b_rows(q):
        return pl.ds(pl.multiple_of(q * 2 * mp, 2 * mp), 2 * mp)

    def project(j, size):
        wj_copy(j, size).wait()
        partial[:, tile(j, size)] = jnp.dot(lhs[...], wj[:, tile(j, size)], preferred_element_type=F32)
        for d in range(1, em):
            q = lax.rem(my + d, em)
            remote(
                partial.at[b_rows(q), tile(j, size)],
                partial_in.at[my, :, tile(j, size)],
                b_ssem.at[d, j],
                b_rsem.at[my, j],
                me,
                q,
            ).start()

    @pl.loop(0, full)
    def _(j):
        project(j, JOINED_TILE)

        @pl.when(j < pairs)
        def _():
            wo_copy(j, 0).start()
            wo_copy(j, 1).start()

    if rest:
        project(full, rest)

    @pl.loop(min(full, pairs), pairs)
    def _(j):
        wo_copy(j, 0).start()
        wo_copy(j, 1).start()

    stride = rows_out.shape[0] // (2 * mp)

    def collect(j, size):
        for d in range(1, em):
            q = lax.rem(my + d, em)
            remote(
                partial.at[b_rows(q), tile(j, size)],
                partial_in.at[q, :, tile(j, size)],
                b_ssem.at[d, j],
                b_rsem.at[q, j],
                me,
                q,
            ).wait()
        total_here = partial[b_rows(my), tile(j, size)]
        for d in range(1, em):
            total_here += partial_in[lax.rem(my + d, em), :, tile(j, size)]
        total_here = total_here.astype(BF16).astype(F32)
        for c in range(size // LANES):
            rows_out[pl.ds(j * (JOINED_TILE // LANES) + c, 2 * mp, stride=stride), :] = total_here[
                :, c * LANES : (c + 1) * LANES
            ]

    for j in range(full):
        collect(j, JOINED_TILE)
    if rest:
        collect(full, rest)

    def c_rows(p):
        return pl.ds(pl.multiple_of(p * 2 * stride, 2 * stride), 2 * stride)

    for d in range(1, mp):
        p = lax.rem(me + d, mp)
        remote(rows_out.at[c_rows(p), :], rows_in.at[me], c_ssem.at[d], c_rsem.at[me], p, my).start()
    rows_in[me] = rows_out[c_rows(me), :]
    for d in range(1, mp):
        p = lax.rem(me + d, mp)
        remote(rows_out.at[c_rows(p), :], rows_in.at[p], c_ssem.at[d], c_rsem.at[p], p, my).wait()

    key_load.wait()
    value_load.wait()
    scale = 1.0 / math.sqrt(dh)
    base = query.shape[0] // 2
    for r in range(2):
        for s in range(mp):
            query[pl.ds(r * base + s * chunks, stride), :] = rows_in[s, r * stride : (r + 1) * stride, :]
    for r in range(2):
        at = r * base
        q32 = jnp.concatenate(
            [query[pl.ds(at, heads, stride=2), :], query[pl.ds(at + 1, heads, stride=2), :]], axis=1
        )
        end = at + 2 * heads
        new_key = jnp.concatenate([query[end : end + 1, :], query[end + 1 : end + 2, :]], axis=1)
        new_value = jnp.concatenate([query[end + 2 : end + 3, :], query[end + 3 : end + 4, :]], axis=1)
        scores = (
            lax.dot_general(
                q32.astype(BF16), keys[r], (((1,), (1,)), ((), ())), preferred_element_type=F32
            )
            * scale
        )
        new_score = jnp.sum(q32 * new_key, axis=1, keepdims=True) * scale
        visible = lax.broadcasted_iota(jnp.int32, (heads, cache_len), 1) < lengths_ref[r]
        scores = jnp.where(visible, scores, -1e30)
        highest = jnp.maximum(jnp.max(scores, axis=1, keepdims=True), new_score)
        expo = jnp.where(visible, jnp.exp(scores - highest), 0.0)
        new_expo = jnp.exp(new_score - highest)
        denominator = jnp.sum(expo, axis=1, keepdims=True) + new_expo
        weights = (expo / denominator).astype(BF16)
        new_weight = (new_expo / denominator).astype(BF16).astype(F32)
        attended = jnp.dot(weights, values[r], preferred_element_type=F32) + new_weight * new_value
        for side in range(2):
            att[...] = attended[:, side * LANES : (side + 1) * LANES]
            for p in range(mp):
                first = (p * 2 + r) * 2 * heads_here + side * heads_here
                att_rows[pl.ds(first, heads_here), :] = att[pl.ds(p * heads_here, heads_here), :]
    att_out[...] = att_rows[...].astype(BF16)

    block = 4 * heads_here

    def d_rows(t):
        return pl.ds(pl.multiple_of(t * block, block), block)

    def d_copy(d, t_slot, s_slot):
        t = lax.rem(own + d, count)
        p, q = t // em, lax.rem(t, em)
        return remote(
            att_out.at[d_rows(p), :],
            att_in.at[d_rows(t_slot), :],
            d_ssem.at[d],
            d_rsem.at[s_slot],
            p,
            q,
        )

    @pl.loop(1, count)
    def _(d):
        d_copy(d, own, own).start()

    att_in[d_rows(own), :] = att_out[d_rows(me), :]

    @pl.loop(1, count)
    def _(d):
        t = lax.rem(own + d, count)
        d_copy(d, t, t).wait()

    att_f32[...] = att_in[...].astype(F32)
    for h in range(heads_here):
        for side in range(2):
            place = (2 * h + side) * LANES
            att_lhs[:, place : place + LANES] = att_f32[
                pl.ds(side * heads_here + h, 2 * count, stride=2 * heads_here), :
            ].astype(BF16)

    def f_rows(p):
        return pl.ds(pl.multiple_of(p * rows_x, rows_x), rows_x)

    def f_copy(d, j, p, slot):
        place = pl.ds(pl.multiple_of(j * OUT_TILE, LANES), OUT_TILE)
        return remote(
            out_send.at[p, :, place], out_in.at[slot, :, place], f_ssem.at[d, j], f_rsem.at[slot, j], p, my
        )

    @pl.loop(0, pairs)
    def _(j):
        here = [
            pl.ds(pl.multiple_of(side * out_half + j * OUT_TILE, LANES), OUT_TILE) for side in range(2)
        ]
        for side in range(2):
            wo_copy(j, side).wait()
            product[:, here[side]] = jnp.dot(
                att_lhs[...], wo[:, here[side]], preferred_element_type=F32
            )
        for d in range(1, mp):
            p = lax.rem(me + d, mp)
            out_send[p, :, pl.ds(pl.multiple_of(j * OUT_TILE, LANES), OUT_TILE)] = jnp.concatenate(
                [product[f_rows(p), here[0]], product[f_rows(p), here[1]]], axis=0
            ).astype(BF16)
            f_copy(d, j, p, me).start()

    @pl.loop(0, pairs)
    def _(j):
        place = pl.ds(pl.multiple_of(j * OUT_TILE, LANES), OUT_TILE)
        here = [
            pl.ds(pl.multiple_of(side * out_half + j * OUT_TILE, LANES), OUT_TILE) for side in range(2)
        ]
        acc = jnp.concatenate([product[f_rows(me), here[0]], product[f_rows(me), here[1]]], axis=0)
        for d in range(1, mp):
            p = lax.rem(me + d, mp)
            f_copy(d, j, p, p).wait()
            acc += out_in[p, :, place].astype(F32)
        out_ref[:, here[0]] = acc[:rows_x].astype(BF16)
        out_ref[:, here[1]] = acc[rows_x:].astype(BF16)

    for d in range(1, mp):
        p = lax.rem(me + d, mp)
        remote(x_pack, x_slot(me), x_ssem.at[d], x_rsem.at[me], p, my).wait_send()


def fused_body(x_rows, joined_weight, cache_keys, cache_values, lengths, out_weight):
    mp = lax.axis_size("mp")
    em = lax.axis_size("embed")
    rows_x, width = x_rows.shape
    _, cache_len, dh = cache_keys.shape
    columns = joined_weight.shape[1]
    features, out_width = out_weight.shape
    heads = features * mp // dh
    chunks = columns // LANES
    stride = -(-chunks // 8) * 8
    total = mp * rows_x
    count = mp * em
    tiles = -(-columns // JOINED_TILE)
    pairs = out_width // 2 // OUT_TILE
    block = 4 * (heads // mp)
    dma = pltpu.SemaphoreType.DMA
    scratch = [
        pltpu.VMEM((rows_x, width), BF16),
        pltpu.VMEM((2 * rows_x, width // 2), BF16),
        pltpu.VMEM((2 * total, width // 2), BF16),
        pltpu.VMEM((total, width), BF16),
        pltpu.VMEM(joined_weight.shape, BF16),
        pltpu.VMEM(out_weight.shape, BF16),
        pltpu.VMEM(cache_keys.shape, BF16),
        pltpu.VMEM(cache_values.shape, BF16),
        pltpu.VMEM((total, columns), F32),
        pltpu.VMEM((em, 2 * mp, columns), F32),
        pltpu.VMEM((2 * mp * stride, LANES), F32),
        pltpu.VMEM((mp, 2 * stride, LANES), F32),
        pltpu.VMEM((2 * (mp * chunks // 8 * 8 + stride), LANES), F32),
        pltpu.VMEM((heads, LANES), F32),
        pltpu.VMEM((mp * block, LANES), F32),
        pltpu.VMEM((mp * block, LANES), BF16),
        pltpu.VMEM((count * block, LANES), BF16),
        pltpu.VMEM((count * block, LANES), F32),
        pltpu.VMEM((total, features), BF16),
        pltpu.VMEM((total, out_width), F32),
        pltpu.VMEM((mp, 2 * rows_x, out_width // 2), BF16),
        pltpu.VMEM((mp, 2 * rows_x, out_width // 2), BF16),
        dma((3,)),
        dma((tiles,)),
        dma((2, pairs)),
        dma((mp,)),
        dma((mp,)),
        dma((em, tiles)),
        dma((em, tiles)),
        dma((mp,)),
        dma((mp,)),
        dma((count,)),
        dma((count,)),
        dma((mp, pairs)),
        dma((mp, pairs)),
    ]
    hbm = pl.BlockSpec(memory_space=pl.ANY)
    return pl.pallas_call(
        functools.partial(fused_kernel, (mp, em, heads, dh, cache_len)),
        out_shape=jax.ShapeDtypeStruct((rows_x, out_width), BF16),
        in_specs=[pl.BlockSpec(memory_space=pltpu.SMEM)] + [hbm] * 5,
        out_specs=pl.BlockSpec(memory_space=pltpu.VMEM),
        scratch_shapes=scratch,
        compiler_params=pltpu.CompilerParams(
            collective_id=0, has_side_effects=True, vmem_limit_bytes=VMEM_BYTES
        ),
    )(lengths, x_rows, joined_weight, cache_keys, cache_values, out_weight)


def plain_body(x_rows, joined_weight, cache_keys, cache_values, lengths, out_weight):
    mp_count = lax.axis_size("mp")
    embed_count = lax.axis_size("embed")
    rows_here = cache_keys.shape[0]
    cache_len = cache_keys.shape[1]
    head_dim = cache_keys.shape[2]
    local_columns = joined_weight.shape[1]
    partial_sums = jnp.dot(
        lax.all_gather(x_rows, "mp", axis=0, tiled=True),
        joined_weight,
        preferred_element_type=jnp.float32,
    )
    shaped = partial_sums.reshape(mp_count, embed_count, rows_here, local_columns)
    summed = lax.psum_scatter(shaped, "embed", scatter_dimension=1, tiled=True).astype(jnp.bfloat16)
    arrived = lax.all_to_all(summed, "mp", split_axis=0, concat_axis=3, tiled=True)
    projected = arrived.reshape(rows_here, local_columns * mp_count)
    query_width = projected.shape[1] - 2 * head_dim
    head_count = query_width // head_dim
    queries = projected[:, :query_width].reshape(rows_here, head_count, head_dim)
    new_key = projected[:, query_width : query_width + head_dim]
    new_value = projected[:, query_width + head_dim :]
    score_scale = 1.0 / math.sqrt(head_dim)
    scores = (
        jnp.einsum("rhd,rld->rhl", queries, cache_keys, preferred_element_type=jnp.float32)
        * score_scale
    )
    new_score = (
        jnp.einsum("rhd,rd->rh", queries, new_key, preferred_element_type=jnp.float32) * score_scale
    )
    visible = jnp.arange(cache_len, dtype=jnp.int32)[None, None, :] < lengths[:, None, None]
    scores = jnp.where(visible, scores, -1e30)
    highest = jnp.maximum(jnp.max(scores, axis=-1), new_score)
    expo = jnp.where(visible, jnp.exp(scores - highest[..., None]), 0.0)
    new_expo = jnp.exp(new_score - highest)
    denominator = jnp.sum(expo, axis=-1) + new_expo
    weights = (expo / denominator[..., None]).astype(jnp.bfloat16)
    new_weight = (new_expo / denominator).astype(jnp.bfloat16)
    attended = jnp.einsum("rhl,rld->rhd", weights, cache_values, preferred_element_type=jnp.float32)
    attended = (
        attended
        + new_weight.astype(jnp.float32)[..., None] * new_value.astype(jnp.float32)[:, None, :]
    )
    attended = attended.astype(jnp.bfloat16).reshape(rows_here, mp_count, query_width // mp_count)
    returned = lax.all_to_all(attended, "mp", split_axis=1, concat_axis=0, tiled=True)
    returned = returned.reshape(mp_count, 1, rows_here, query_width // mp_count)
    partial_out = jnp.einsum(
        "ikrw,wd->ikrd",
        lax.all_gather(returned, "embed", axis=1, tiled=True),
        out_weight,
        preferred_element_type=jnp.float32,
    )
    partial_out = partial_out.reshape(mp_count * embed_count * rows_here, out_weight.shape[1])
    result = lax.psum_scatter(partial_out, "mp", scatter_dimension=0, tiled=True)
    return result.astype(jnp.bfloat16)


def body(x_rows, joined_weight, cache_keys, cache_values, lengths, out_weight):
    mp = lax.axis_size("mp")
    em = lax.axis_size("embed")
    rows_x, width = x_rows.shape
    rows_here, _, dh = cache_keys.shape
    columns = joined_weight.shape[1]
    features, out_width = out_weight.shape
    held = 2 * (joined_weight.size + out_weight.size + cache_keys.size + cache_values.size)
    fits = (
        rows_here == 2
        and rows_x == 8
        and em * 2 == rows_x
        and mp * 2 == 8
        and dh == 2 * LANES
        and columns % LANES == 0
        and width % (2 * LANES) == 0
        and features % dh == 0
        and (features // dh) % 4 == 0
        and out_width % (2 * OUT_TILE) == 0
        and held < VMEM_BYTES - 6 * 1024 * 1024
    )
    chosen = fused_body if fits else plain_body
    return chosen(x_rows, joined_weight, cache_keys, cache_values, lengths, out_weight)


def solution(mesh):
    return jax.shard_map(
        body,
        mesh=mesh,
        in_specs=(
            P(("groups", "mp"), "embed"),
            P("embed", "mp"),
            P(("groups", "mp", "embed"), None, None),
            P(("groups", "mp", "embed"), None, None),
            P(("groups", "mp", "embed")),
            P("mp", "embed"),
        ),
        out_specs=P(("groups", "mp"), "embed"),
        check_vma=False,
    )
```

```python
import functools
import math

import jax
import jax.numpy as jnp
from jax import lax
from jax.experimental import pallas as pl
from jax.experimental.pallas import tpu as pltpu
from jax.sharding import PartitionSpec as P


LANES = 128
JOINED_TILE = 512
OUT_TILE = 768
GROUP = 4
F32 = jnp.float32
BF16 = jnp.bfloat16
VMEM_BYTES = 63 * 1024 * 1024


def fused_kernel(
    sizes,
    lengths_ref,
    x_ref,
    wj_ref,
    ck_ref,
    cv_ref,
    wo_ref,
    out_ref,
    x_in,
    x_pack,
    x_all,
    lhs,
    wj,
    wo,
    keys,
    values,
    partial,
    partial_in,
    rows_out,
    rows_in,
    query,
    att,
    att_rows,
    att_out,
    att_in,
    att_f32,
    att_lhs,
    product,
    out_send,
    out_in,
    load_sem,
    wj_sem,
    wo_sem,
    x_ssem,
    x_rsem,
    b_ssem,
    b_rsem,
    c_ssem,
    c_rsem,
    d_ssem,
    d_rsem,
    f_ssem,
    f_rsem,
):
    mp, em, heads, dh, cache_len = sizes
    me = lax.axis_index("mp")
    my = lax.axis_index("embed")
    count = mp * em
    own = me * em + my
    rows_x, width = x_ref.shape
    half = width // 2
    columns = wj_ref.shape[1]
    chunks = columns // LANES
    full = columns // JOINED_TILE
    rest = columns - full * JOINED_TILE
    out_half = out_ref.shape[1] // 2
    pairs = out_half // OUT_TILE
    heads_here = heads // mp
    groups = heads_here // GROUP

    def remote(src, dst, ssem, rsem, p, q):
        return pltpu.make_async_remote_copy(
            src_ref=src,
            dst_ref=dst,
            send_sem=ssem,
            recv_sem=rsem,
            device_id={"mp": p, "embed": q},
            device_id_type=pl.DeviceIdType.MESH,
        )

    def tile(j, size=JOINED_TILE):
        return pl.ds(pl.multiple_of(j * JOINED_TILE, LANES), size)

    def wj_copy(j, size=JOINED_TILE):
        return pltpu.make_async_copy(wj_ref.at[:, tile(j, size)], wj.at[:, tile(j, size)], wj_sem.at[j])

    def wo_copy(j, side):
        place = pl.ds(pl.multiple_of(side * out_half + j * OUT_TILE, LANES), OUT_TILE)
        return pltpu.make_async_copy(wo_ref.at[:, place], wo.at[:, place], wo_sem.at[side, j])

    x_load = pltpu.make_async_copy(x_ref, x_in, load_sem.at[0])
    x_load.start()

    @pl.loop(0, full)
    def _(j):
        wj_copy(j).start()

    if rest:
        wj_copy(full, rest).start()
    key_load = pltpu.make_async_copy(ck_ref, keys, load_sem.at[1])
    value_load = pltpu.make_async_copy(cv_ref, values, load_sem.at[2])
    key_load.start()
    value_load.start()

    barrier = pltpu.get_barrier_semaphore()

    for d in range(1, mp):
        pl.semaphore_signal(
            barrier, inc=1, device_id={"mp": lax.rem(me + d, mp)}, device_id_type=pl.DeviceIdType.MESH
        )
    for d in range(1, em):
        pl.semaphore_signal(
            barrier, inc=1, device_id={"embed": lax.rem(my + d, em)}, device_id_type=pl.DeviceIdType.MESH
        )

    x_load.wait()
    x32 = x_in[...].astype(F32)
    x_pack[...] = jnp.concatenate([x32[:, :half], x32[:, half:]], axis=0).astype(BF16)
    pl.semaphore_wait(barrier, mp + em - 2)

    def x_slot(p):
        return x_all.at[pl.ds(pl.multiple_of(p * 2 * rows_x, 2 * rows_x), 2 * rows_x), :]

    core = lax.rem(me, 2)
    beside = me + 1 - 2 * core
    across = lax.rem(me + 2, mp)
    diagonal = lax.rem(beside + 2, mp)
    send_across = remote(x_pack, x_slot(me), x_ssem.at[1], x_rsem.at[1], across, my)
    send_beside = remote(x_pack, x_slot(me), x_ssem.at[0], x_rsem.at[0], beside, my)
    relay = remote(x_slot(across), x_slot(across), x_ssem.at[2], x_rsem.at[2], beside, my)
    send_across.start()
    send_beside.start()
    x_slot(me)[...] = x_pack[...]
    remote(x_pack, x_slot(across), x_ssem.at[1], x_rsem.at[1], across, my).wait_recv()
    relay.start()
    remote(x_pack, x_slot(beside), x_ssem.at[0], x_rsem.at[0], beside, my).wait_recv()
    remote(x_pack, x_slot(diagonal), x_ssem.at[2], x_rsem.at[2], beside, my).wait_recv()

    total = mp * rows_x
    row = lax.broadcasted_iota(jnp.int32, (total, 2 * total), 0)
    col = lax.broadcasted_iota(jnp.int32, (total, 2 * total), 1)
    wanted = (lax.rem(row, 2 * mp) // 2) * (2 * rows_x) + (row // (2 * mp)) * 2 + lax.rem(row, 2)
    for side in range(2):
        pick = jnp.where(col == wanted + side * rows_x, 1.0, 0.0).astype(BF16)
        lhs[:, side * half : (side + 1) * half] = jnp.dot(
            pick, x_all[...], preferred_element_type=F32
        ).astype(BF16)

    def b_rows(q):
        return pl.ds(pl.multiple_of(q * 2 * mp, 2 * mp), 2 * mp)

    def project(j, size):
        wj_copy(j, size).wait()
        partial[:, tile(j, size)] = jnp.dot(lhs[...], wj[:, tile(j, size)], preferred_element_type=F32)
        for d in range(1, em):
            q = lax.rem(my + d, em)
            remote(
                partial.at[b_rows(q), tile(j, size)],
                partial_in.at[my, :, tile(j, size)],
                b_ssem.at[d, j],
                b_rsem.at[my, j],
                me,
                q,
            ).start()

    @pl.loop(0, full)
    def _(j):
        project(j, JOINED_TILE)

        @pl.when(j < pairs)
        def _():
            wo_copy(j, 0).start()
            wo_copy(j, 1).start()

    if rest:
        project(full, rest)

    @pl.loop(min(full, pairs), pairs)
    def _(j):
        wo_copy(j, 0).start()
        wo_copy(j, 1).start()

    stride = rows_out.shape[0] // (2 * mp)

    def collect(j, size):
        for d in range(1, em):
            q = lax.rem(my + d, em)
            remote(
                partial.at[b_rows(q), tile(j, size)],
                partial_in.at[q, :, tile(j, size)],
                b_ssem.at[d, j],
                b_rsem.at[q, j],
                me,
                q,
            ).wait()
        total_here = partial[b_rows(my), tile(j, size)]
        for d in range(1, em):
            total_here += partial_in[lax.rem(my + d, em), :, tile(j, size)]
        total_here = total_here.astype(BF16).astype(F32)
        for c in range(size // LANES):
            rows_out[pl.ds(j * (JOINED_TILE // LANES) + c, 2 * mp, stride=stride), :] = total_here[
                :, c * LANES : (c + 1) * LANES
            ]

    for j in range(full):
        collect(j, JOINED_TILE)
    if rest:
        collect(full, rest)

    def c_rows(p):
        return pl.ds(pl.multiple_of(p * 2 * stride, 2 * stride), 2 * stride)

    for d in range(1, mp):
        p = lax.rem(me + d, mp)
        remote(rows_out.at[c_rows(p), :], rows_in.at[me], c_ssem.at[d], c_rsem.at[me], p, my).start()
    rows_in[me] = rows_out[c_rows(me), :]
    for d in range(1, mp):
        p = lax.rem(me + d, mp)
        remote(rows_out.at[c_rows(p), :], rows_in.at[p], c_ssem.at[d], c_rsem.at[p], p, my).wait()

    key_load.wait()
    value_load.wait()
    scale = 1.0 / math.sqrt(dh)
    base = query.shape[0] // 2
    for r in range(2):
        for s in range(mp):
            query[pl.ds(r * base + s * chunks, stride), :] = rows_in[s, r * stride : (r + 1) * stride, :]
    for r in range(2):
        at = r * base
        q32 = jnp.concatenate(
            [query[pl.ds(at, heads, stride=2), :], query[pl.ds(at + 1, heads, stride=2), :]], axis=1
        )
        end = at + 2 * heads
        new_key = jnp.concatenate([query[end : end + 1, :], query[end + 1 : end + 2, :]], axis=1)
        new_value = jnp.concatenate([query[end + 2 : end + 3, :], query[end + 3 : end + 4, :]], axis=1)
        scores = (
            lax.dot_general(
                q32.astype(BF16), keys[r], (((1,), (1,)), ((), ())), preferred_element_type=F32
            )
            * scale
        )
        new_score = jnp.sum(q32 * new_key, axis=1, keepdims=True) * scale
        visible = lax.broadcasted_iota(jnp.int32, (heads, cache_len), 1) < lengths_ref[r]
        scores = jnp.where(visible, scores, -1e30)
        highest = jnp.maximum(jnp.max(scores, axis=1, keepdims=True), new_score)
        expo = jnp.where(visible, jnp.exp(scores - highest), 0.0)
        new_expo = jnp.exp(new_score - highest)
        denominator = jnp.sum(expo, axis=1, keepdims=True) + new_expo
        weights = (expo / denominator).astype(BF16)
        new_weight = (new_expo / denominator).astype(BF16).astype(F32)
        attended = jnp.dot(weights, values[r], preferred_element_type=F32) + new_weight * new_value
        for side in range(2):
            att[...] = attended[:, side * LANES : (side + 1) * LANES]
            for g in range(groups):
                for p in range(mp):
                    first = ((g * mp + p) * 2 + r) * 2 * GROUP + side * GROUP
                    att_rows[pl.ds(first, GROUP), :] = att[pl.ds(p * heads_here + g * GROUP, GROUP), :]
    att_out[...] = att_rows[...].astype(BF16)

    block = 4 * GROUP

    def d_rows(t):
        return pl.ds(pl.multiple_of(t * block, block), block)

    def d_copy(g, d, slot):
        t = lax.rem(own + d, count)
        p, q = t // em, lax.rem(t, em)
        return remote(
            att_out.at[d_rows(g * mp + p), :],
            att_in.at[d_rows(g * count + slot), :],
            d_ssem.at[g, d],
            d_rsem.at[g, slot],
            p,
            q,
        )

    @pl.loop(0, groups)
    def _(g):
        @pl.loop(1, count)
        def _(d):
            d_copy(g, d, own).start()

    for g in range(groups):
        att_in[d_rows(g * count + own), :] = att_out[d_rows(g * mp + me), :]

    def f_rows(p):
        return pl.ds(pl.multiple_of(p * rows_x, rows_x), rows_x)

    def f_copy(d, j, p, slot):
        place = pl.ds(pl.multiple_of(j * OUT_TILE, LANES), OUT_TILE)
        return remote(
            out_send.at[p, :, place], out_in.at[slot, :, place], f_ssem.at[d, j], f_rsem.at[slot, j], p, my
        )

    for g in range(groups):

        @pl.loop(1, count)
        def _(d):
            d_copy(g, d, lax.rem(own + d, count)).wait()

        rows = pl.ds(g * count * block, count * block)
        att_f32[...] = att_in[rows, :].astype(F32)
        for h in range(GROUP):
            for side in range(2):
                place = (2 * h + side) * LANES
                att_lhs[:, place : place + LANES] = att_f32[
                    pl.ds(side * GROUP + h, 2 * count, stride=2 * GROUP), :
                ].astype(BF16)
        depth = pl.ds(g * GROUP * dh, GROUP * dh)

        @pl.loop(0, pairs)
        def _(j):
            here = [
                pl.ds(pl.multiple_of(side * out_half + j * OUT_TILE, LANES), OUT_TILE) for side in range(2)
            ]
            for side in range(2):
                if g == 0:
                    wo_copy(j, side).wait()
                term = jnp.dot(att_lhs[...], wo[depth, here[side]], preferred_element_type=F32)
                if g == 0:
                    product[:, here[side]] = term
                else:
                    product[:, here[side]] += term
            if g == groups - 1:
                for d in range(1, mp):
                    p = lax.rem(me + d, mp)
                    out_send[p, :, pl.ds(pl.multiple_of(j * OUT_TILE, LANES), OUT_TILE)] = jnp.concatenate(
                        [product[f_rows(p), here[0]], product[f_rows(p), here[1]]], axis=0
                    ).astype(BF16)
                    f_copy(d, j, p, me).start()

    @pl.loop(0, pairs)
    def _(j):
        place = pl.ds(pl.multiple_of(j * OUT_TILE, LANES), OUT_TILE)
        here = [
            pl.ds(pl.multiple_of(side * out_half + j * OUT_TILE, LANES), OUT_TILE) for side in range(2)
        ]
        acc = jnp.concatenate([product[f_rows(me), here[0]], product[f_rows(me), here[1]]], axis=0)
        for d in range(1, mp):
            p = lax.rem(me + d, mp)
            f_copy(d, j, p, p).wait()
            acc += out_in[p, :, place].astype(F32)
        out_ref[:, here[0]] = acc[:rows_x].astype(BF16)
        out_ref[:, here[1]] = acc[rows_x:].astype(BF16)

    send_across.wait_send()
    send_beside.wait_send()
    relay.wait_send()


def fused_body(x_rows, joined_weight, cache_keys, cache_values, lengths, out_weight):
    mp = lax.axis_size("mp")
    em = lax.axis_size("embed")
    rows_x, width = x_rows.shape
    _, cache_len, dh = cache_keys.shape
    columns = joined_weight.shape[1]
    features, out_width = out_weight.shape
    heads = features * mp // dh
    chunks = columns // LANES
    stride = -(-chunks // 8) * 8
    total = mp * rows_x
    count = mp * em
    tiles = -(-columns // JOINED_TILE)
    pairs = out_width // 2 // OUT_TILE
    block = 4 * (heads // mp)
    dma = pltpu.SemaphoreType.DMA
    scratch = [
        pltpu.VMEM((rows_x, width), BF16),
        pltpu.VMEM((2 * rows_x, width // 2), BF16),
        pltpu.VMEM((2 * total, width // 2), BF16),
        pltpu.VMEM((total, width), BF16),
        pltpu.VMEM(joined_weight.shape, BF16),
        pltpu.VMEM(out_weight.shape, BF16),
        pltpu.VMEM(cache_keys.shape, BF16),
        pltpu.VMEM(cache_values.shape, BF16),
        pltpu.VMEM((total, columns), F32),
        pltpu.VMEM((em, 2 * mp, columns), F32),
        pltpu.VMEM((2 * mp * stride, LANES), F32),
        pltpu.VMEM((mp, 2 * stride, LANES), F32),
        pltpu.VMEM((2 * (mp * chunks // 8 * 8 + stride), LANES), F32),
        pltpu.VMEM((heads, LANES), F32),
        pltpu.VMEM((mp * block, LANES), F32),
        pltpu.VMEM((mp * block, LANES), BF16),
        pltpu.VMEM((count * block, LANES), BF16),
        pltpu.VMEM((4 * GROUP * count, LANES), F32),
        pltpu.VMEM((total, GROUP * dh), BF16),
        pltpu.VMEM((total, out_width), F32),
        pltpu.VMEM((mp, 2 * rows_x, out_width // 2), BF16),
        pltpu.VMEM((mp, 2 * rows_x, out_width // 2), BF16),
        dma((3,)),
        dma((tiles,)),
        dma((2, pairs)),
        dma((mp,)),
        dma((mp,)),
        dma((em, tiles)),
        dma((em, tiles)),
        dma((mp,)),
        dma((mp,)),
        dma((heads // mp // GROUP, count)),
        dma((heads // mp // GROUP, count)),
        dma((mp, pairs)),
        dma((mp, pairs)),
    ]
    hbm = pl.BlockSpec(memory_space=pl.ANY)
    return pl.pallas_call(
        functools.partial(fused_kernel, (mp, em, heads, dh, cache_len)),
        out_shape=jax.ShapeDtypeStruct((rows_x, out_width), BF16),
        in_specs=[pl.BlockSpec(memory_space=pltpu.SMEM)] + [hbm] * 5,
        out_specs=pl.BlockSpec(memory_space=pltpu.VMEM),
        scratch_shapes=scratch,
        compiler_params=pltpu.CompilerParams(
            collective_id=0, has_side_effects=True, vmem_limit_bytes=VMEM_BYTES
        ),
    )(lengths, x_rows, joined_weight, cache_keys, cache_values, out_weight)


def plain_body(x_rows, joined_weight, cache_keys, cache_values, lengths, out_weight):
    mp_count = lax.axis_size("mp")
    embed_count = lax.axis_size("embed")
    rows_here = cache_keys.shape[0]
    cache_len = cache_keys.shape[1]
    head_dim = cache_keys.shape[2]
    local_columns = joined_weight.shape[1]
    partial_sums = jnp.dot(
        lax.all_gather(x_rows, "mp", axis=0, tiled=True),
        joined_weight,
        preferred_element_type=jnp.float32,
    )
    shaped = partial_sums.reshape(mp_count, embed_count, rows_here, local_columns)
    summed = lax.psum_scatter(shaped, "embed", scatter_dimension=1, tiled=True).astype(jnp.bfloat16)
    arrived = lax.all_to_all(summed, "mp", split_axis=0, concat_axis=3, tiled=True)
    projected = arrived.reshape(rows_here, local_columns * mp_count)
    query_width = projected.shape[1] - 2 * head_dim
    head_count = query_width // head_dim
    queries = projected[:, :query_width].reshape(rows_here, head_count, head_dim)
    new_key = projected[:, query_width : query_width + head_dim]
    new_value = projected[:, query_width + head_dim :]
    score_scale = 1.0 / math.sqrt(head_dim)
    scores = (
        jnp.einsum("rhd,rld->rhl", queries, cache_keys, preferred_element_type=jnp.float32)
        * score_scale
    )
    new_score = (
        jnp.einsum("rhd,rd->rh", queries, new_key, preferred_element_type=jnp.float32) * score_scale
    )
    visible = jnp.arange(cache_len, dtype=jnp.int32)[None, None, :] < lengths[:, None, None]
    scores = jnp.where(visible, scores, -1e30)
    highest = jnp.maximum(jnp.max(scores, axis=-1), new_score)
    expo = jnp.where(visible, jnp.exp(scores - highest[..., None]), 0.0)
    new_expo = jnp.exp(new_score - highest)
    denominator = jnp.sum(expo, axis=-1) + new_expo
    weights = (expo / denominator[..., None]).astype(jnp.bfloat16)
    new_weight = (new_expo / denominator).astype(jnp.bfloat16)
    attended = jnp.einsum("rhl,rld->rhd", weights, cache_values, preferred_element_type=jnp.float32)
    attended = (
        attended
        + new_weight.astype(jnp.float32)[..., None] * new_value.astype(jnp.float32)[:, None, :]
    )
    attended = attended.astype(jnp.bfloat16).reshape(rows_here, mp_count, query_width // mp_count)
    returned = lax.all_to_all(attended, "mp", split_axis=1, concat_axis=0, tiled=True)
    returned = returned.reshape(mp_count, 1, rows_here, query_width // mp_count)
    partial_out = jnp.einsum(
        "ikrw,wd->ikrd",
        lax.all_gather(returned, "embed", axis=1, tiled=True),
        out_weight,
        preferred_element_type=jnp.float32,
    )
    partial_out = partial_out.reshape(mp_count * embed_count * rows_here, out_weight.shape[1])
    result = lax.psum_scatter(partial_out, "mp", scatter_dimension=0, tiled=True)
    return result.astype(jnp.bfloat16)


def body(x_rows, joined_weight, cache_keys, cache_values, lengths, out_weight):
    mp = lax.axis_size("mp")
    em = lax.axis_size("embed")
    rows_x, width = x_rows.shape
    rows_here, _, dh = cache_keys.shape
    columns = joined_weight.shape[1]
    features, out_width = out_weight.shape
    held = 2 * (joined_weight.size + out_weight.size + cache_keys.size + cache_values.size)
    fits = (
        rows_here == 2
        and rows_x == 8
        and em * 2 == rows_x
        and mp * 2 == 8
        and dh == 2 * LANES
        and columns % LANES == 0
        and width % (2 * LANES) == 0
        and features % dh == 0
        and (features // dh) % GROUP == 0
        and out_width % (2 * OUT_TILE) == 0
        and held < VMEM_BYTES - 6 * 1024 * 1024
    )
    chosen = fused_body if fits else plain_body
    return chosen(x_rows, joined_weight, cache_keys, cache_values, lengths, out_weight)


def solution(mesh):
    return jax.shard_map(
        body,
        mesh=mesh,
        in_specs=(
            P(("groups", "mp"), "embed"),
            P("embed", "mp"),
            P(("groups", "mp", "embed"), None, None),
            P(("groups", "mp", "embed"), None, None),
            P(("groups", "mp", "embed")),
            P("mp", "embed"),
        ),
        out_specs=P(("groups", "mp"), "embed"),
        check_vma=False,
    )
```

```python
import functools
import math

import jax
import jax.numpy as jnp
from jax import lax
from jax.experimental import pallas as pl
from jax.experimental.pallas import tpu as pltpu
from jax.sharding import PartitionSpec as P


LANES = 128
JOINED_TILE = 640
OUT_TILE = 1152
GROUP = 4
F32 = jnp.float32
BF16 = jnp.bfloat16
VMEM_BYTES = 63 * 1024 * 1024


def fused_kernel(
    sizes,
    lengths_ref,
    x_ref,
    wj_ref,
    ck_ref,
    cv_ref,
    wo_ref,
    out_ref,
    x_in,
    x_pack,
    x_all,
    lhs,
    wj,
    wo,
    keys,
    values,
    partial,
    partial_in,
    rows_out,
    rows_in,
    query,
    att,
    att_rows,
    att_out,
    att_in,
    att_f32,
    att_lhs,
    product,
    out_send,
    out_in,
    load_sem,
    wj_sem,
    wo_sem,
    x_ssem,
    x_rsem,
    b_ssem,
    b_rsem,
    c_ssem,
    c_rsem,
    d_ssem,
    d_rsem,
    f_ssem,
    f_rsem,
):
    mp, em, heads, dh, cache_len = sizes
    me = lax.axis_index("mp")
    my = lax.axis_index("embed")
    count = mp * em
    own = me * em + my
    rows_x, width = x_ref.shape
    half = width // 2
    columns = wj_ref.shape[1]
    chunks = columns // LANES
    full = columns // JOINED_TILE
    rest = columns - full * JOINED_TILE
    out_half = out_ref.shape[1] // 2
    pairs = out_half // OUT_TILE
    heads_here = heads // mp
    groups = heads_here // GROUP

    def remote(src, dst, ssem, rsem, p, q):
        return pltpu.make_async_remote_copy(
            src_ref=src,
            dst_ref=dst,
            send_sem=ssem,
            recv_sem=rsem,
            device_id={"mp": p, "embed": q},
            device_id_type=pl.DeviceIdType.MESH,
        )

    def tile(j, size=JOINED_TILE):
        return pl.ds(pl.multiple_of(j * JOINED_TILE, LANES), size)

    def wj_copy(j, size=JOINED_TILE):
        return pltpu.make_async_copy(wj_ref.at[:, tile(j, size)], wj.at[:, tile(j, size)], wj_sem.at[j])

    def wo_copy(j, side):
        place = pl.ds(pl.multiple_of(side * out_half + j * OUT_TILE, LANES), OUT_TILE)
        return pltpu.make_async_copy(wo_ref.at[:, place], wo.at[:, place], wo_sem.at[side, j])

    x_load = pltpu.make_async_copy(x_ref, x_in, load_sem.at[0])
    x_load.start()

    @pl.loop(0, full)
    def _(j):
        wj_copy(j).start()

    if rest:
        wj_copy(full, rest).start()
    key_load = pltpu.make_async_copy(ck_ref, keys, load_sem.at[1])
    value_load = pltpu.make_async_copy(cv_ref, values, load_sem.at[2])
    key_load.start()
    value_load.start()

    barrier = pltpu.get_barrier_semaphore()

    for d in range(1, mp):
        pl.semaphore_signal(
            barrier, inc=1, device_id={"mp": lax.rem(me + d, mp)}, device_id_type=pl.DeviceIdType.MESH
        )
    for d in range(1, em):
        pl.semaphore_signal(
            barrier, inc=1, device_id={"embed": lax.rem(my + d, em)}, device_id_type=pl.DeviceIdType.MESH
        )

    x_load.wait()
    x32 = x_in[...].astype(F32)
    x_pack[...] = jnp.concatenate([x32[:, :half], x32[:, half:]], axis=0).astype(BF16)
    pl.semaphore_wait(barrier, mp + em - 2)

    def x_slot(p):
        return x_all.at[pl.ds(pl.multiple_of(p * 2 * rows_x, 2 * rows_x), 2 * rows_x), :]

    core = lax.rem(me, 2)
    beside = me + 1 - 2 * core
    across = lax.rem(me + 2, mp)
    diagonal = lax.rem(beside + 2, mp)
    send_across = remote(x_pack, x_slot(me), x_ssem.at[1], x_rsem.at[1], across, my)
    send_beside = remote(x_pack, x_slot(me), x_ssem.at[0], x_rsem.at[0], beside, my)
    relay = remote(x_slot(across), x_slot(across), x_ssem.at[2], x_rsem.at[2], beside, my)
    send_across.start()
    send_beside.start()
    x_slot(me)[...] = x_pack[...]
    remote(x_pack, x_slot(across), x_ssem.at[1], x_rsem.at[1], across, my).wait_recv()
    relay.start()
    remote(x_pack, x_slot(beside), x_ssem.at[0], x_rsem.at[0], beside, my).wait_recv()
    remote(x_pack, x_slot(diagonal), x_ssem.at[2], x_rsem.at[2], beside, my).wait_recv()

    total = mp * rows_x
    row = lax.broadcasted_iota(jnp.int32, (total, 2 * total), 0)
    col = lax.broadcasted_iota(jnp.int32, (total, 2 * total), 1)
    wanted = (lax.rem(row, 2 * mp) // 2) * (2 * rows_x) + (row // (2 * mp)) * 2 + lax.rem(row, 2)
    for side in range(2):
        pick = jnp.where(col == wanted + side * rows_x, 1.0, 0.0).astype(BF16)
        lhs[:, side * half : (side + 1) * half] = jnp.dot(
            pick, x_all[...], preferred_element_type=F32
        ).astype(BF16)

    def b_rows(q):
        return pl.ds(pl.multiple_of(q * 2 * mp, 2 * mp), 2 * mp)

    def project(j, size):
        wj_copy(j, size).wait()
        partial[:, tile(j, size)] = jnp.dot(lhs[...], wj[:, tile(j, size)], preferred_element_type=F32)
        for d in range(1, em):
            q = lax.rem(my + d, em)
            remote(
                partial.at[b_rows(q), tile(j, size)],
                partial_in.at[my, :, tile(j, size)],
                b_ssem.at[d, j],
                b_rsem.at[my, j],
                me,
                q,
            ).start()

    @pl.loop(0, full)
    def _(j):
        project(j, JOINED_TILE)

        @pl.when(j < pairs)
        def _():
            wo_copy(j, 0).start()
            wo_copy(j, 1).start()

    if rest:
        project(full, rest)

    @pl.loop(min(full, pairs), pairs)
    def _(j):
        wo_copy(j, 0).start()
        wo_copy(j, 1).start()

    stride = rows_out.shape[0] // (2 * mp)

    def collect(j, size):
        for d in range(1, em):
            q = lax.rem(my + d, em)
            remote(
                partial.at[b_rows(q), tile(j, size)],
                partial_in.at[q, :, tile(j, size)],
                b_ssem.at[d, j],
                b_rsem.at[q, j],
                me,
                q,
            ).wait()
        total_here = partial[b_rows(my), tile(j, size)]
        for d in range(1, em):
            total_here += partial_in[lax.rem(my + d, em), :, tile(j, size)]
        total_here = total_here.astype(BF16).astype(F32)
        for c in range(size // LANES):
            rows_out[pl.ds(j * (JOINED_TILE // LANES) + c, 2 * mp, stride=stride), :] = total_here[
                :, c * LANES : (c + 1) * LANES
            ]

    for j in range(full):
        collect(j, JOINED_TILE)
    if rest:
        collect(full, rest)

    def c_rows(p):
        return pl.ds(pl.multiple_of(p * 2 * stride, 2 * stride), 2 * stride)

    for d in range(1, mp):
        p = lax.rem(me + d, mp)
        remote(rows_out.at[c_rows(p), :], rows_in.at[me], c_ssem.at[d], c_rsem.at[me], p, my).start()
    rows_in[me] = rows_out[c_rows(me), :]
    for d in range(1, mp):
        p = lax.rem(me + d, mp)
        remote(rows_out.at[c_rows(p), :], rows_in.at[p], c_ssem.at[d], c_rsem.at[p], p, my).wait()

    key_load.wait()
    value_load.wait()
    scale = 1.0 / math.sqrt(dh)
    base = query.shape[0] // 2
    for r in range(2):
        for s in range(mp):
            query[pl.ds(r * base + s * chunks, stride), :] = rows_in[s, r * stride : (r + 1) * stride, :]
    for r in range(2):
        at = r * base
        q32 = jnp.concatenate(
            [query[pl.ds(at, heads, stride=2), :], query[pl.ds(at + 1, heads, stride=2), :]], axis=1
        )
        end = at + 2 * heads
        new_key = jnp.concatenate([query[end : end + 1, :], query[end + 1 : end + 2, :]], axis=1)
        new_value = jnp.concatenate([query[end + 2 : end + 3, :], query[end + 3 : end + 4, :]], axis=1)
        scores = (
            lax.dot_general(
                q32.astype(BF16), keys[r], (((1,), (1,)), ((), ())), preferred_element_type=F32
            )
            * scale
        )
        new_score = jnp.sum(q32 * new_key, axis=1, keepdims=True) * scale
        visible = lax.broadcasted_iota(jnp.int32, (heads, cache_len), 1) < lengths_ref[r]
        scores = jnp.where(visible, scores, -1e30)
        highest = jnp.maximum(jnp.max(scores, axis=1, keepdims=True), new_score)
        expo = jnp.where(visible, jnp.exp(scores - highest), 0.0)
        new_expo = jnp.exp(new_score - highest)
        denominator = jnp.sum(expo, axis=1, keepdims=True) + new_expo
        weights = (expo / denominator).astype(BF16)
        new_weight = (new_expo / denominator).astype(BF16).astype(F32)
        attended = jnp.dot(weights, values[r], preferred_element_type=F32) + new_weight * new_value
        for side in range(2):
            att[...] = attended[:, side * LANES : (side + 1) * LANES]
            for g in range(groups):
                for p in range(mp):
                    first = ((g * mp + p) * 2 + r) * 2 * GROUP + side * GROUP
                    att_rows[pl.ds(first, GROUP), :] = att[pl.ds(p * heads_here + g * GROUP, GROUP), :]
    att_out[...] = att_rows[...].astype(BF16)

    block = 4 * GROUP

    def d_rows(t):
        return pl.ds(pl.multiple_of(t * block, block), block)

    def d_copy(g, d, slot):
        t = lax.rem(own + d, count)
        p, q = t // em, lax.rem(t, em)
        return remote(
            att_out.at[d_rows(g * mp + p), :],
            att_in.at[d_rows(g * count + slot), :],
            d_ssem.at[g, d],
            d_rsem.at[g, slot],
            p,
            q,
        )

    @pl.loop(0, groups)
    def _(g):
        @pl.loop(1, count)
        def _(d):
            d_copy(g, d, own).start()

    for g in range(groups):
        att_in[d_rows(g * count + own), :] = att_out[d_rows(g * mp + me), :]

    def f_rows(p):
        return pl.ds(pl.multiple_of(p * rows_x, rows_x), rows_x)

    def f_copy(d, j, p, slot):
        place = pl.ds(pl.multiple_of(j * OUT_TILE, LANES), OUT_TILE)
        return remote(
            out_send.at[p, :, place], out_in.at[slot, :, place], f_ssem.at[d, j], f_rsem.at[slot, j], p, my
        )

    for g in range(groups):

        @pl.loop(1, count)
        def _(d):
            d_copy(g, d, lax.rem(own + d, count)).wait()

        rows = pl.ds(g * count * block, count * block)
        att_f32[...] = att_in[rows, :].astype(F32)
        for h in range(GROUP):
            for side in range(2):
                place = (2 * h + side) * LANES
                att_lhs[:, place : place + LANES] = att_f32[
                    pl.ds(side * GROUP + h, 2 * count, stride=2 * GROUP), :
                ].astype(BF16)
        depth = pl.ds(g * GROUP * dh, GROUP * dh)

        @pl.loop(0, pairs)
        def _(j):
            here = [
                pl.ds(pl.multiple_of(side * out_half + j * OUT_TILE, LANES), OUT_TILE) for side in range(2)
            ]
            for side in range(2):
                if g == 0:
                    wo_copy(j, side).wait()
                term = jnp.dot(att_lhs[...], wo[depth, here[side]], preferred_element_type=F32)
                if g == 0:
                    product[:, here[side]] = term
                else:
                    product[:, here[side]] += term
            if g == groups - 1:
                for d in (2, 1, 3):
                    p = lax.rem(me + d, mp)
                    out_send[p, :, pl.ds(pl.multiple_of(j * OUT_TILE, LANES), OUT_TILE)] = jnp.concatenate(
                        [product[f_rows(p), here[0]], product[f_rows(p), here[1]]], axis=0
                    ).astype(BF16)
                    f_copy(d, j, p, me).start()

    @pl.loop(0, pairs)
    def _(j):
        place = pl.ds(pl.multiple_of(j * OUT_TILE, LANES), OUT_TILE)
        here = [
            pl.ds(pl.multiple_of(side * out_half + j * OUT_TILE, LANES), OUT_TILE) for side in range(2)
        ]
        acc = jnp.concatenate([product[f_rows(me), here[0]], product[f_rows(me), here[1]]], axis=0)
        for d in range(1, mp):
            p = lax.rem(me + d, mp)
            f_copy(d, j, p, p).wait()
            acc += out_in[p, :, place].astype(F32)
        out_ref[:, here[0]] = acc[:rows_x].astype(BF16)
        out_ref[:, here[1]] = acc[rows_x:].astype(BF16)

    send_across.wait_send()
    send_beside.wait_send()
    relay.wait_send()


def fused_body(x_rows, joined_weight, cache_keys, cache_values, lengths, out_weight):
    mp = lax.axis_size("mp")
    em = lax.axis_size("embed")
    rows_x, width = x_rows.shape
    _, cache_len, dh = cache_keys.shape
    columns = joined_weight.shape[1]
    features, out_width = out_weight.shape
    heads = features * mp // dh
    chunks = columns // LANES
    stride = -(-chunks // 8) * 8
    total = mp * rows_x
    count = mp * em
    tiles = -(-columns // JOINED_TILE)
    pairs = out_width // 2 // OUT_TILE
    block = 4 * (heads // mp)
    dma = pltpu.SemaphoreType.DMA
    scratch = [
        pltpu.VMEM((rows_x, width), BF16),
        pltpu.VMEM((2 * rows_x, width // 2), BF16),
        pltpu.VMEM((2 * total, width // 2), BF16),
        pltpu.VMEM((total, width), BF16),
        pltpu.VMEM(joined_weight.shape, BF16),
        pltpu.VMEM(out_weight.shape, BF16),
        pltpu.VMEM(cache_keys.shape, BF16),
        pltpu.VMEM(cache_values.shape, BF16),
        pltpu.VMEM((total, columns), F32),
        pltpu.VMEM((em, 2 * mp, columns), F32),
        pltpu.VMEM((2 * mp * stride, LANES), F32),
        pltpu.VMEM((mp, 2 * stride, LANES), F32),
        pltpu.VMEM((2 * (mp * chunks // 8 * 8 + stride), LANES), F32),
        pltpu.VMEM((heads, LANES), F32),
        pltpu.VMEM((mp * block, LANES), F32),
        pltpu.VMEM((mp * block, LANES), BF16),
        pltpu.VMEM((count * block, LANES), BF16),
        pltpu.VMEM((4 * GROUP * count, LANES), F32),
        pltpu.VMEM((total, GROUP * dh), BF16),
        pltpu.VMEM((total, out_width), F32),
        pltpu.VMEM((mp, 2 * rows_x, out_width // 2), BF16),
        pltpu.VMEM((mp, 2 * rows_x, out_width // 2), BF16),
        dma((3,)),
        dma((tiles,)),
        dma((2, pairs)),
        dma((mp,)),
        dma((mp,)),
        dma((em, tiles)),
        dma((em, tiles)),
        dma((mp,)),
        dma((mp,)),
        dma((heads // mp // GROUP, count)),
        dma((heads // mp // GROUP, count)),
        dma((mp, pairs)),
        dma((mp, pairs)),
    ]
    hbm = pl.BlockSpec(memory_space=pl.ANY)
    return pl.pallas_call(
        functools.partial(fused_kernel, (mp, em, heads, dh, cache_len)),
        out_shape=jax.ShapeDtypeStruct((rows_x, out_width), BF16),
        in_specs=[pl.BlockSpec(memory_space=pltpu.SMEM)] + [hbm] * 5,
        out_specs=pl.BlockSpec(memory_space=pltpu.VMEM),
        scratch_shapes=scratch,
        compiler_params=pltpu.CompilerParams(
            collective_id=0, has_side_effects=True, vmem_limit_bytes=VMEM_BYTES
        ),
    )(lengths, x_rows, joined_weight, cache_keys, cache_values, out_weight)


def plain_body(x_rows, joined_weight, cache_keys, cache_values, lengths, out_weight):
    mp_count = lax.axis_size("mp")
    embed_count = lax.axis_size("embed")
    rows_here = cache_keys.shape[0]
    cache_len = cache_keys.shape[1]
    head_dim = cache_keys.shape[2]
    local_columns = joined_weight.shape[1]
    partial_sums = jnp.dot(
        lax.all_gather(x_rows, "mp", axis=0, tiled=True),
        joined_weight,
        preferred_element_type=jnp.float32,
    )
    shaped = partial_sums.reshape(mp_count, embed_count, rows_here, local_columns)
    summed = lax.psum_scatter(shaped, "embed", scatter_dimension=1, tiled=True).astype(jnp.bfloat16)
    arrived = lax.all_to_all(summed, "mp", split_axis=0, concat_axis=3, tiled=True)
    projected = arrived.reshape(rows_here, local_columns * mp_count)
    query_width = projected.shape[1] - 2 * head_dim
    head_count = query_width // head_dim
    queries = projected[:, :query_width].reshape(rows_here, head_count, head_dim)
    new_key = projected[:, query_width : query_width + head_dim]
    new_value = projected[:, query_width + head_dim :]
    score_scale = 1.0 / math.sqrt(head_dim)
    scores = (
        jnp.einsum("rhd,rld->rhl", queries, cache_keys, preferred_element_type=jnp.float32)
        * score_scale
    )
    new_score = (
        jnp.einsum("rhd,rd->rh", queries, new_key, preferred_element_type=jnp.float32) * score_scale
    )
    visible = jnp.arange(cache_len, dtype=jnp.int32)[None, None, :] < lengths[:, None, None]
    scores = jnp.where(visible, scores, -1e30)
    highest = jnp.maximum(jnp.max(scores, axis=-1), new_score)
    expo = jnp.where(visible, jnp.exp(scores - highest[..., None]), 0.0)
    new_expo = jnp.exp(new_score - highest)
    denominator = jnp.sum(expo, axis=-1) + new_expo
    weights = (expo / denominator[..., None]).astype(jnp.bfloat16)
    new_weight = (new_expo / denominator).astype(jnp.bfloat16)
    attended = jnp.einsum("rhl,rld->rhd", weights, cache_values, preferred_element_type=jnp.float32)
    attended = (
        attended
        + new_weight.astype(jnp.float32)[..., None] * new_value.astype(jnp.float32)[:, None, :]
    )
    attended = attended.astype(jnp.bfloat16).reshape(rows_here, mp_count, query_width // mp_count)
    returned = lax.all_to_all(attended, "mp", split_axis=1, concat_axis=0, tiled=True)
    returned = returned.reshape(mp_count, 1, rows_here, query_width // mp_count)
    partial_out = jnp.einsum(
        "ikrw,wd->ikrd",
        lax.all_gather(returned, "embed", axis=1, tiled=True),
        out_weight,
        preferred_element_type=jnp.float32,
    )
    partial_out = partial_out.reshape(mp_count * embed_count * rows_here, out_weight.shape[1])
    result = lax.psum_scatter(partial_out, "mp", scatter_dimension=0, tiled=True)
    return result.astype(jnp.bfloat16)


def body(x_rows, joined_weight, cache_keys, cache_values, lengths, out_weight):
    mp = lax.axis_size("mp")
    em = lax.axis_size("embed")
    rows_x, width = x_rows.shape
    rows_here, _, dh = cache_keys.shape
    columns = joined_weight.shape[1]
    features, out_width = out_weight.shape
    held = 2 * (joined_weight.size + out_weight.size + cache_keys.size + cache_values.size)
    fits = (
        rows_here == 2
        and rows_x == 8
        and em * 2 == rows_x
        and mp * 2 == 8
        and dh == 2 * LANES
        and columns % LANES == 0
        and width % (2 * LANES) == 0
        and features % dh == 0
        and (features // dh) % GROUP == 0
        and out_width % (2 * OUT_TILE) == 0
        and held < VMEM_BYTES - 6 * 1024 * 1024
    )
    chosen = fused_body if fits else plain_body
    return chosen(x_rows, joined_weight, cache_keys, cache_values, lengths, out_weight)


def solution(mesh):
    return jax.shard_map(
        body,
        mesh=mesh,
        in_specs=(
            P(("groups", "mp"), "embed"),
            P("embed", "mp"),
            P(("groups", "mp", "embed"), None, None),
            P(("groups", "mp", "embed"), None, None),
            P(("groups", "mp", "embed")),
            P("mp", "embed"),
        ),
        out_specs=P(("groups", "mp"), "embed"),
        check_vma=False,
    )
```
